32 devices in a mesh: groups: 2 (over y), facet: 4 (over z), subband: 4 (over x, core).
Axes of the slice: x: 2, y: 2, z: 4, core: 2. Of those that a mesh axis runs over, the one named last changes fastest.
Arguments:
- model: bfloat16 [8192, 2048], P(('groups', 'facet')), parts along dimension 0, may hold values from -6 to 6
- kernel: bfloat16 [2048, 128], P('subband'), may hold values from -0.125 to 0.125
- spectrum: float32 [8, 128], P(('groups', 'subband')), parts along dimension 0, may hold values from 0.5 to 2
- observed: bfloat16 [8, 16, 512, 128], P(('groups', 'subband'), 'facet'), parts along dimension 0, may hold values from -6 to 6
- subgrid_ids: int32 [8, 512], P('groups'), parts along dimension 0, may hold values from 0 to 4095
- owners: int32 [8], P('groups'), parts along dimension 0, may hold values from 0 to 3
Outputs:
- residual: bfloat16 [8, 2048, 128], P(('groups', 'subband')), parts along dimension 0
- dirty: bfloat16 [8192, 2048], P(('groups', 'facet', 'subband')), parts along dimension 0
The draws below stay inside these ranges and needn't reach their ends.
There are 2 independent parts, one for each index of `groups`. The reference program is written for one: setup_inputs(seed, part) draws one part's arguments, and reference() takes and returns one part's arrays. A program takes and returns all parts, laid end to end along the dimension named above; an argument that names none is the same for every part. Nothing has to cross between parts.
All inputs are finite; a program needn't handle non-finite values.
Results may differ from the reference program's by a relative error of at most 0.0095.
Values may be sent and summed in bfloat16 or wider, within the bound.
A program may use at most 64 MiB of HBM per device.

```python
import math
import jax
import jax.numpy as jnp
from jax import lax

PIX = 2048
VB = 128
NBLK = 512
SPANS = 4
SUBS = 4096
SUBBANDS = 4
N_FACET = 4


def set_ends(drawn, rng, least, high):
    longest = drawn.shape.index(max(drawn.shape))
    spots = []
    for shift in (0, 1):
        where = [jax.random.randint(jax.random.fold_in(rng, axis), (), 0, length) for axis, length in enumerate(drawn.shape)]
        where[longest] = (where[longest] + shift) % drawn.shape[longest]
        spots.append(tuple(where))
    return drawn.at[spots[0]].set(least).at[spots[1]].set(high)


def steps_of(own_key, shape, split, least, top_value):
    def one(dim, shards_of):
        heights = jax.random.uniform(jax.random.fold_in(jax.random.fold_in(own_key, 6), dim), (shards_of,), jnp.float32, least / len(split), top_value / len(split))
        return jnp.repeat(jnp.exp(heights), shape[dim] // shards_of).reshape((-1,) + (1,) * (len(shape) - dim - 1))

    gain = one(*split[0])
    for cut in split[1:]:
        gain = gain * one(*cut)
    return gain


def noise(stream_key, dims, spread, limit, cuts=(), kind=jnp.bfloat16):
    result = jax.random.normal(stream_key, dims, jnp.float32) * spread
    if len(cuts) > 0:
        result = steps_of(stream_key, dims, cuts, -0.22, 0.18) * result
    return jnp.clip(result, min=-limit, max=limit).astype(kind)


def setup_inputs(seed: int = 0, part: int = 0) -> dict:
    keys = jax.random.split(jax.random.key(seed), 7)
    part_splits = jax.random.split(jax.random.fold_in(keys[6], part), 7)
    return {
        "model": noise(part_splits[0], (SUBS, PIX), 1.0, 6.0, ((0, 4),)),
        "kernel": noise(keys[1], (PIX, VB), PIX ** -0.5, 0.125, ((0, 4),)),
        "spectrum": jnp.clip(jnp.exp(math.log(2.0) - 1.3862944 * jax.random.uniform(part_splits[2], (SUBBANDS, VB), jnp.float32) ** steps_of(part_splits[2], (SUBBANDS, VB), ((0, 4),), -0.2, 0.2)), 0.5, 2.0),
        "observed": noise(part_splits[3], (SUBBANDS, N_FACET * SPANS, NBLK, VB), 1.0, 6.0, ((0, 4), (1, 4))),
        "subgrid_ids": set_ends(jax.random.randint(part_splits[4], (SPANS, NBLK), 0, SUBS), jax.random.fold_in(part_splits[4], 1), 0, SUBS - 1).astype(jnp.int32),
        "owners": set_ends(jax.random.randint(part_splits[5], (SPANS,), 0, N_FACET), jax.random.fold_in(part_splits[5], 1), 0, N_FACET - 1).astype(jnp.int32),
    }


def reference(model, kernel, spectrum, observed, subgrid_ids, owners):
    predicted = jnp.dot(model, kernel, preferred_element_type=jnp.float32).astype(jnp.bfloat16)
    predicted = lax.optimization_barrier(predicted).astype(jnp.float32)
    flat_ids = subgrid_ids.reshape(-1).astype(jnp.int32)
    rows = predicted[flat_ids]
    positions = (owners * SPANS + jnp.arange(SPANS, dtype=jnp.int32)).astype(jnp.int32)
    chosen = observed[:, positions].reshape(SUBBANDS, SPANS * NBLK, VB).astype(jnp.float32)
    residual = (chosen - rows[None, :, :] * spectrum[:, None, :]).astype(jnp.bfloat16)
    grids = jax.vmap(lambda r: jax.ops.segment_sum(r.astype(jnp.float32), flat_ids, SUBS))(residual)
    weighted = (grids * spectrum[:, None, :]).astype(jnp.bfloat16)
    weighted = lax.optimization_barrier(weighted).astype(jnp.float32)
    total = jnp.sum(weighted, axis=0)
    dirty = jnp.dot(total, kernel.astype(jnp.float32).T, precision=lax.Precision.HIGHEST)
    return residual, dirty.astype(jnp.bfloat16)
```

```python
import functools

import jax
import jax.numpy as jnp
from jax import lax
from jax.experimental import pallas as pl
from jax.experimental.pallas import tpu as pltpu
from jax.sharding import PartitionSpec as P

MESH = pl.DeviceIdType.MESH
F32 = jnp.float32
BF16 = jnp.bfloat16
CHUNK = 256
LAG = 1


def remote(src, dst, send, recv, axis, target):
    return pltpu.make_async_remote_copy(
        src_ref=src, dst_ref=dst, send_sem=send, recv_sem=recv,
        device_id={axis: target}, device_id_type=MESH,
    )


def body(nf, ns, model, kernel, spectrum, observed, ids, owners, residual, dirty,
         model_v, kern, acc, pred, vals, r_in, l_in, r_out, l_out, res, grid, wsend, wrecv, dout,
         msem, ks, kr, rs, rr, ls, lr, ws, wr, osem, dsem):
    z = lax.axis_index("facet")
    s = lax.axis_index("subband")
    nx = ns // 2
    mate = s + 1 - 2 * (s % 2)
    subs, depth = model_v.shape[1], model_v.shape[2]
    spans, nblk = ids.shape
    per = nblk // CHUNK
    chunks = spans * per
    width = kernel.shape[1]

    order = [s, mate]
    for d in range(1, nx):
        order += [(s + ns - 2 * d) % ns, (mate + ns - 2 * d) % ns]
    loads = []
    for n, k in enumerate(order):
        at = pl.multiple_of(k * depth, depth)
        loads.append(pltpu.make_async_copy(model.at[:, pl.ds(at, depth)], model_v.at[n], msem.at[n]))
        loads[-1].start()

    barrier = pltpu.get_barrier_semaphore()
    for d in range(1, ns):
        pl.semaphore_signal(barrier, inc=1, device_id={"subband": (s + d) % ns}, device_id_type=MESH)

    @pl.when(z > 0)
    def _():
        pl.semaphore_signal(barrier, inc=1, device_id={"facet": z - 1}, device_id_type=MESH)

    @pl.when(z < nf - 1)
    def _():
        pl.semaphore_signal(barrier, inc=1, device_id={"facet": z + 1}, device_id_type=MESH)

    has_left = jnp.where(z > 0, 1, 0)
    has_right = jnp.where(z < nf - 1, 1, 0)
    pl.semaphore_wait(barrier, ns - 1 + has_left + has_right)

    cross = []
    for d in range(1, nx):
        c = remote(kernel, kern.at[s], ks.at[d], kr.at[d], "subband", (s + 2 * d) % ns)
        c.start()
        cross.append(c)
    near = remote(kernel, kern.at[s], ks.at[0], kr.at[0], "subband", mate)
    near.start()
    kern[s] = kernel[...]

    def add(n, k):
        loads[n].wait()
        part = jnp.dot(model_v[n], kern[k], preferred_element_type=F32)
        acc[...] = part if n == 0 else acc[...] + part

    add(0, s)
    near.wait_recv()
    add(1, mate)
    passed = []
    for d in range(1, nx):
        src = (s + ns - 2 * d) % ns
        cross[d - 1].wait_recv()
        c = remote(kern.at[src], kern.at[src], ks.at[nx + d - 1], kr.at[nx + d - 1], "subband", mate)
        c.start()
        passed.append(c)
        add(2 * d, src)
    for d in range(1, nx):
        passed[d - 1].wait_recv()
        add(2 * d + 1, (mate + ns - 2 * d) % ns)
    pred[...] = acc[...].astype(BF16)

    spec = spectrum[...]
    offset = z * subs
    grid[...] = jnp.zeros_like(grid)

    def right(i):
        return remote(r_out.at[i], r_in.at[i], rs.at[i], rr.at[i], "facet", z + 1)

    def left(i):
        return remote(l_out.at[i], l_in.at[i], ls.at[i], lr.at[i], "facet", z - 1)

    def out(i):
        at = pl.multiple_of(i * CHUNK, CHUNK)
        return pltpu.make_async_copy(res.at[i], residual.at[0, pl.ds(at, CHUNK)], osem.at[i])

    def step(t, _):
        @pl.when(t < chunks)
        def _():
            span = t // per
            row = ids[pl.ds(span, 1), pl.ds(pl.multiple_of((t % per) * CHUNK, CHUNK), CHUNK)] - offset
            column = jnp.broadcast_to(row, (128, CHUNK)).T
            lanes = lax.broadcasted_iota(jnp.int32, (CHUNK, 128), 1)
            pick = jnp.concatenate(
                [(column == lanes + 128 * j).astype(F32).astype(BF16) for j in range(subs // 128)], axis=1
            )
            rows = jnp.dot(pick, pred[...], preferred_element_type=F32)
            mine = jnp.where(owners[span] == z, 1.0, 0.0).astype(F32)
            seen = observed[0, span, pl.ds(pl.multiple_of((t % per) * CHUNK, CHUNK), CHUNK), :]
            vals[t] = seen.astype(F32) * mine - rows * spec

        i = t - LAG * z
        @pl.when(jnp.logical_and(i >= 0, i < chunks))
        def _():
            @pl.when(z == 0)
            def _():
                r_out[i] = vals[i].astype(BF16)

            @pl.when(z > 0)
            def _():
                right(i).wait_recv()
                r_out[i] = (vals[i] + r_in[i].astype(F32)).astype(BF16)

            @pl.when(z < nf - 1)
            def _():
                right(i).start()

        j = t - LAG * (nf - 1 - z)
        @pl.when(jnp.logical_and(j >= 0, j < chunks))
        def _():
            @pl.when(z == nf - 1)
            def _():
                l_out[j] = vals[j].astype(BF16)

            @pl.when(z < nf - 1)
            def _():
                left(j).wait_recv()
                l_out[j] = (vals[j] + l_in[j].astype(F32)).astype(BF16)

            @pl.when(z > 0)
            def _():
                left(j).start()

        e = t - LAG * jnp.maximum(z, nf - 1 - z)
        @pl.when(jnp.logical_and(e >= 0, e < chunks))
        def _():
            @pl.when(z == 0)
            def _():
                res[e] = l_out[e]

            @pl.when(z == nf - 1)
            def _():
                res[e] = r_out[e]

            @pl.when(jnp.logical_and(z > 0, z < nf - 1))
            def _():
                res[e] = (vals[e] + (r_in[e].astype(F32) + l_in[e].astype(F32))).astype(BF16)

            out(e).start()
            row = ids[pl.ds(e // per, 1), pl.ds(pl.multiple_of((e % per) * CHUNK, CHUNK), CHUNK)] - offset
            place = (lax.broadcasted_iota(jnp.int32, (subs, CHUNK), 0) == row).astype(F32).astype(BF16)
            grid[...] += jnp.dot(place, res[e], preferred_element_type=F32)

        return 0

    lax.fori_loop(0, chunks + LAG * (nf - 1), step, 0)

    share = subs // ns
    wsend[...] = (grid[...] * spec).astype(BF16)
    parts = []
    for d in range(1, ns):
        to = (s + d) % ns
        at = pl.multiple_of(to * share, share)
        c = remote(wsend.at[pl.ds(at, share)], wrecv.at[d - 1], ws.at[d - 1], wr.at[d - 1], "subband", to)
        c.start()
        parts.append(c)
    total = wsend[pl.ds(pl.multiple_of(s * share, share), share), :].astype(F32)
    for d in range(1, ns):
        parts[d - 1].wait_recv()
        total = total + wrecv[d - 1].astype(F32)
    high = total.astype(BF16)
    low = (total - high.astype(F32)).astype(BF16)
    back = (((1,), (1,)), ((), ()))
    stores = []
    for k in range(ns):
        block = lax.dot_general(high, kern[k], back, preferred_element_type=F32)
        block += lax.dot_general(low, kern[k], back, preferred_element_type=F32)
        dout[k] = block.astype(BF16)
        c = pltpu.make_async_copy(dout.at[k], dirty.at[:, pl.ds(k * depth, depth)], dsem.at[k])
        c.start()
        stores.append(c)

    for c in [near] + cross + passed + parts:
        c.wait_send()

    def drain(i, _):
        @pl.when(z < nf - 1)
        def _():
            right(i).wait_send()

        @pl.when(z > 0)
        def _():
            left(i).wait_send()

        out(i).wait()
        return 0

    lax.fori_loop(0, chunks, drain, 0)
    for c in stores:
        c.wait()


def local(nf, ns, model, kernel, spectrum, observed, subgrid_ids, owners):
    subs, pix = model.shape
    depth, width = kernel.shape
    spans, nblk = subgrid_ids.shape
    chunks = spans * nblk // CHUNK
    share = subs // ns
    dma = pltpu.SemaphoreType.DMA
    vmem = pl.BlockSpec(memory_space=pltpu.VMEM)
    anywhere = pl.BlockSpec(memory_space=pl.ANY)
    flow = pltpu.VMEM((chunks, CHUNK, width), BF16)
    return pl.pallas_call(
        functools.partial(body, nf, ns),
        out_shape=(
            jax.ShapeDtypeStruct((1, spans * nblk, width), BF16),
            jax.ShapeDtypeStruct((share, pix), BF16),
        ),
        in_specs=[anywhere, vmem, vmem, vmem, vmem, pl.BlockSpec(memory_space=pltpu.SMEM)],
        out_specs=(anywhere, anywhere),
        scratch_shapes=[
            pltpu.VMEM((ns, subs, depth), BF16),
            pltpu.VMEM((ns, depth, width), BF16),
            pltpu.VMEM((subs, width), F32),
            pltpu.VMEM((subs, width), BF16),
            pltpu.VMEM((chunks, CHUNK, width), F32),
            flow, flow, flow, flow, flow,
            pltpu.VMEM((subs, width), F32),
            pltpu.VMEM((subs, width), BF16),
            pltpu.VMEM((ns - 1, share, width), BF16),
            pltpu.VMEM((ns, share, depth), BF16),
            dma((ns,)),
            dma((ns,)), dma((ns,)),
            dma((chunks,)), dma((chunks,)), dma((chunks,)), dma((chunks,)),
            dma((ns - 1,)), dma((ns - 1,)),
            dma((chunks,)), dma((ns,)),
        ],
        compiler_params=pltpu.CompilerParams(
            collective_id=0, has_side_effects=True, vmem_limit_bytes=40 * 1024 * 1024
        ),
        name="major_cycle",
    )(model, kernel, spectrum, observed, subgrid_ids, owners)


def solution(mesh):
    return jax.shard_map(
        functools.partial(local, mesh.shape["facet"], mesh.shape["subband"]),
        mesh=mesh,
        in_specs=(
            P(("groups", "facet"), None),
            P("subband", None),
            P(("groups", "subband"), None),
            P(("groups", "subband"), "facet", None, None),
            P("groups", None),
            P("groups"),
        ),
        out_specs=(P(("groups", "subband"), None, None), P(("groups", "facet", "subband"), None)),
        check_vma=False,
    )
```

```python
import functools

import jax
import jax.numpy as jnp
from jax import lax
from jax.experimental import pallas as pl
from jax.experimental.pallas import tpu as pltpu
from jax.sharding import PartitionSpec as P

MESH = pl.DeviceIdType.MESH
F32 = jnp.float32
BF16 = jnp.bfloat16
CHUNK = 128
LAG = 5


def remote(src, dst, send, recv, axis, target):
    return pltpu.make_async_remote_copy(
        src_ref=src, dst_ref=dst, send_sem=send, recv_sem=recv,
        device_id={axis: target}, device_id_type=MESH,
    )


def body(nf, ns, model, kernel_h, spectrum, observed, ids_h, owners_h, residual, dirty,
         kernel, ids, owners, spec_v, small,
         model_v, kern, acc, pred, vals, r_in, l_in, r_out, l_out, res, grid, wsend, wrecv, dout,
         ids_v, obs_v, obsem, msem, ks, kr, rs, rr, ls, lr, ws, wr, osem, dsem):
    z = lax.axis_index("facet")
    s = lax.axis_index("subband")
    nx = ns // 2
    mate = s + 1 - 2 * (s % 2)
    subs, depth = model_v.shape[1], model_v.shape[2]
    spans, nblk = ids.shape
    per = nblk // CHUNK
    chunks = spans * per
    width = kernel.shape[1]

    first = pltpu.make_async_copy(kernel_h, kernel, small.at[0])
    first.start()
    others = [
        pltpu.make_async_copy(ids_h, ids, small.at[1]),
        pltpu.make_async_copy(owners_h, owners, small.at[2]),
        pltpu.make_async_copy(spectrum, spec_v, small.at[3]),
    ]
    for c in others:
        c.start()

    order = [s, mate]
    for d in range(1, nx):
        order += [(s + ns - 2 * d) % ns, (mate + ns - 2 * d) % ns]
    loads = []
    for n, k in enumerate(order):
        at = pl.multiple_of(k * depth, depth)
        loads.append(pltpu.make_async_copy(model.at[:, pl.ds(at, depth)], model_v.at[n], msem.at[n]))
        loads[-1].start()

    seen_load = pltpu.make_async_copy(observed.at[0], obs_v, obsem)
    seen_load.start()
    barrier = pltpu.get_barrier_semaphore()
    for d in range(1, ns):
        pl.semaphore_signal(barrier, inc=1, device_id={"subband": (s + d) % ns}, device_id_type=MESH)

    @pl.when(z > 0)
    def _():
        pl.semaphore_signal(barrier, inc=1, device_id={"facet": z - 1}, device_id_type=MESH)

    @pl.when(z < nf - 1)
    def _():
        pl.semaphore_signal(barrier, inc=1, device_id={"facet": z + 1}, device_id_type=MESH)

    has_left = jnp.where(z > 0, 1, 0)
    has_right = jnp.where(z < nf - 1, 1, 0)
    pl.semaphore_wait(barrier, ns - 1 + has_left + has_right)

    first.wait()
    cross = []
    for d in range(1, nx):
        c = remote(kernel, kern.at[s], ks.at[d], kr.at[d], "subband", (s + 2 * d) % ns)
        c.start()
        cross.append(c)
    near = remote(kernel, kern.at[s], ks.at[0], kr.at[0], "subband", mate)
    near.start()
    kern[s] = kernel[...]

    def add(n, k):
        loads[n].wait()
        part = jnp.dot(model_v[n], kern[k], preferred_element_type=F32)
        acc[...] = part if n == 0 else acc[...] + part

    add(0, s)
    near.wait_recv()
    add(1, mate)
    passed = []
    for d in range(1, nx):
        src = (s + ns - 2 * d) % ns
        cross[d - 1].wait_recv()
        c = remote(kern.at[src], kern.at[src], ks.at[nx + d - 1], kr.at[nx + d - 1], "subband", mate)
        c.start()
        passed.append(c)
        add(2 * d, src)
    for d in range(1, nx):
        passed[d - 1].wait_recv()
        add(2 * d + 1, (mate + ns - 2 * d) % ns)
    pred[...] = acc[...].astype(BF16)

    for c in others + [seen_load]:
        c.wait()
    spec = spec_v[...]
    for c in range(chunks):
        ids_v[c] = ids[c // per:c // per + 1, c % per * CHUNK:(c % per + 1) * CHUNK]
    offset = z * subs
    grid[...] = jnp.zeros_like(grid)

    def right(i):
        return remote(r_out.at[i], r_in.at[i], rs.at[i], rr.at[i], "facet", z + 1)

    def left(i):
        return remote(l_out.at[i], l_in.at[i], ls.at[i], lr.at[i], "facet", z - 1)

    def out(i):
        at = pl.multiple_of(i * CHUNK, CHUNK)
        return pltpu.make_async_copy(res.at[i], residual.at[0, pl.ds(at, CHUNK)], osem.at[i])

    def step(t, _):
        @pl.when(t < chunks)
        def _():
            span = t // per
            row = ids_v[t] - offset
            column = jnp.broadcast_to(row, (128, CHUNK)).T
            lanes = lax.broadcasted_iota(jnp.int32, (CHUNK, 128), 1)
            pick = jnp.concatenate(
                [(column == lanes + 128 * j).astype(F32).astype(BF16) for j in range(subs // 128)], axis=1
            )
            rows = jnp.dot(pick, pred[...], preferred_element_type=F32)
            mine = jnp.where(owners[span] == z, 1.0, 0.0).astype(F32)
            seen = obs_v[span, pl.ds(pl.multiple_of((t % per) * CHUNK, CHUNK), CHUNK), :]
            vals[t] = seen.astype(F32) * mine - rows * spec

        i = t - LAG * z
        @pl.when(jnp.logical_and(i >= 0, i < chunks))
        def _():
            @pl.when(z == 0)
            def _():
                r_out[i] = vals[i].astype(BF16)

            @pl.when(z > 0)
            def _():
                right(i).wait_recv()
                r_out[i] = (vals[i] + r_in[i].astype(F32)).astype(BF16)

            @pl.when(z < nf - 1)
            def _():
                right(i).start()

        j = t - LAG * (nf - 1 - z)
        @pl.when(jnp.logical_and(j >= 0, j < chunks))
        def _():
            @pl.when(z == nf - 1)
            def _():
                l_out[j] = vals[j].astype(BF16)

            @pl.when(z < nf - 1)
            def _():
                left(j).wait_recv()
                l_out[j] = (vals[j] + l_in[j].astype(F32)).astype(BF16)

            @pl.when(z > 0)
            def _():
                left(j).start()

        e = t - LAG * jnp.maximum(z, nf - 1 - z)
        @pl.when(jnp.logical_and(e >= 0, e < chunks))
        def _():
            @pl.when(z == 0)
            def _():
                res[e] = l_out[e]

            @pl.when(z == nf - 1)
            def _():
                res[e] = r_out[e]

            @pl.when(jnp.logical_and(z > 0, z < nf - 1))
            def _():
                res[e] = (vals[e] + (r_in[e].astype(F32) + l_in[e].astype(F32))).astype(BF16)

            out(e).start()
            row = ids_v[e] - offset
            place = (lax.broadcasted_iota(jnp.int32, (subs, CHUNK), 0) == row).astype(F32).astype(BF16)
            grid[...] += jnp.dot(place, res[e], preferred_element_type=F32)

        return 0

    lax.fori_loop(0, chunks + LAG * (nf - 1), step, 0)

    share = subs // ns
    wsend[...] = (grid[...] * spec).astype(BF16)
    parts = []
    for d in range(1, ns):
        to = (s + d) % ns
        at = pl.multiple_of(to * share, share)
        c = remote(wsend.at[pl.ds(at, share)], wrecv.at[d - 1], ws.at[d - 1], wr.at[d - 1], "subband", to)
        c.start()
        parts.append(c)
    total = wsend[pl.ds(pl.multiple_of(s * share, share), share), :].astype(F32)
    for d in range(1, ns):
        parts[d - 1].wait_recv()
        total = total + wrecv[d - 1].astype(F32)
    high = total.astype(BF16)
    low = (total - high.astype(F32)).astype(BF16)
    back = (((1,), (1,)), ((), ()))
    stores = []
    for k in range(ns):
        block = lax.dot_general(high, kern[k], back, preferred_element_type=F32)
        block += lax.dot_general(low, kern[k], back, preferred_element_type=F32)
        dout[k] = block.astype(BF16)
        c = pltpu.make_async_copy(dout.at[k], dirty.at[:, pl.ds(k * depth, depth)], dsem.at[k])
        c.start()
        stores.append(c)

    for c in [near] + cross + passed + parts:
        c.wait_send()

    def drain(i, _):
        @pl.when(z < nf - 1)
        def _():
            right(i).wait_send()

        @pl.when(z > 0)
        def _():
            left(i).wait_send()

        out(i).wait()
        return 0

    lax.fori_loop(0, chunks, drain, 0)
    for c in stores:
        c.wait()


def local(nf, ns, model, kernel, spectrum, observed, subgrid_ids, owners):
    subs, pix = model.shape
    depth, width = kernel.shape
    spans, nblk = subgrid_ids.shape
    chunks = spans * nblk // CHUNK
    share = subs // ns
    dma = pltpu.SemaphoreType.DMA
    anywhere = pl.BlockSpec(memory_space=pl.ANY)
    flow = pltpu.VMEM((chunks, CHUNK, width), BF16)
    return pl.pallas_call(
        functools.partial(body, nf, ns),
        out_shape=(
            jax.ShapeDtypeStruct((1, spans * nblk, width), BF16),
            jax.ShapeDtypeStruct((share, pix), BF16),
        ),
        in_specs=[anywhere] * 6,
        out_specs=(anywhere, anywhere),
        scratch_shapes=[
            pltpu.VMEM((depth, width), BF16),
            pltpu.VMEM((spans, nblk), jnp.int32),
            pltpu.SMEM(owners.shape, jnp.int32),
            pltpu.VMEM((1, width), F32),
            dma((4,)),
            pltpu.VMEM((ns, subs, depth), BF16),
            pltpu.VMEM((ns, depth, width), BF16),
            pltpu.VMEM((subs, width), F32),
            pltpu.VMEM((subs, width), BF16),
            pltpu.VMEM((chunks, CHUNK, width), F32),
            flow, flow, flow, flow, flow,
            pltpu.VMEM((subs, width), F32),
            pltpu.VMEM((subs, width), BF16),
            pltpu.VMEM((ns - 1, share, width), BF16),
            pltpu.VMEM((ns, share, depth), BF16),
            pltpu.VMEM((chunks, 1, CHUNK), jnp.int32),
            pltpu.VMEM(observed.shape[1:], BF16),
            dma,
            dma((ns,)),
            dma((ns,)), dma((ns,)),
            dma((chunks,)), dma((chunks,)), dma((chunks,)), dma((chunks,)),
            dma((ns - 1,)), dma((ns - 1,)),
            dma((chunks,)), dma((ns,)),
        ],
        compiler_params=pltpu.CompilerParams(
            collective_id=0, has_side_effects=True, vmem_limit_bytes=60 * 1024 * 1024
        ),
        name="major_cycle",
    )(model, kernel, spectrum, observed, subgrid_ids, owners)


def solution(mesh):
    return jax.shard_map(
        functools.partial(local, mesh.shape["facet"], mesh.shape["subband"]),
        mesh=mesh,
        in_specs=(
            P(("groups", "facet"), None),
            P("subband", None),
            P(("groups", "subband"), None),
            P(("groups", "subband"), "facet", None, None),
            P("groups", None),
            P("groups"),
        ),
        out_specs=(P(("groups", "subband"), None, None), P(("groups", "facet", "subband"), None)),
        check_vma=False,
    )
```

```python
import functools

import jax
import jax.numpy as jnp
from jax import lax
from jax.experimental import pallas as pl
from jax.experimental.pallas import tpu as pltpu
from jax.sharding import PartitionSpec as P

MESH = pl.DeviceIdType.MESH
F32 = jnp.float32
BF16 = jnp.bfloat16
CHUNK = 128
GROUP = 4
LAG = 5
EXTRA = 5


def remote(src, dst, send, recv, axis, target):
    return pltpu.make_async_remote_copy(
        src_ref=src, dst_ref=dst, send_sem=send, recv_sem=recv,
        device_id={axis: target}, device_id_type=MESH,
    )


def body(nf, ns, model, kernel_h, spectrum, observed, ids_h, owners_h, residual, total_h, kern_h,
         kernel, ids, owners, spec_v, small,
         model_v, kern, acc, pred, vals, r_in, l_in, r_out, l_out, done, px, grid, wsend, wrecv, total_v,
         ids_v, obs_v, obsem, msem, ks, kr, rs, rr, ls, lr, ps, pr, ws, wr, osem, dsem):
    z = lax.axis_index("facet")
    s = lax.axis_index("subband")
    nx = ns // 2
    mate = s + 1 - 2 * (s % 2)
    subs, depth = model_v.shape[1], model_v.shape[2]
    spans, nblk = ids.shape
    per = nblk // CHUNK
    chunks = spans * per
    early = chunks // 2
    picks = early // ns
    messages = chunks + picks
    width = kernel.shape[1]

    first = pltpu.make_async_copy(kernel_h, kernel, small.at[0])
    first.start()
    others = [
        pltpu.make_async_copy(ids_h, ids, small.at[1]),
        pltpu.make_async_copy(owners_h, owners, small.at[2]),
        pltpu.make_async_copy(spectrum, spec_v, small.at[3]),
    ]
    for c in others:
        c.start()

    order = [s, mate]
    for d in range(1, nx):
        order += [(s + ns - 2 * d) % ns, (mate + ns - 2 * d) % ns]
    loads = []
    for n, k in enumerate(order):
        at = pl.multiple_of(k * depth, depth)
        loads.append(pltpu.make_async_copy(model.at[:, pl.ds(at, depth)], model_v.at[n], msem.at[n]))
        loads[-1].start()

    seen_load = pltpu.make_async_copy(observed.at[0], obs_v, obsem)
    seen_load.start()
    barrier = pltpu.get_barrier_semaphore()
    for d in range(1, ns):
        pl.semaphore_signal(barrier, inc=1, device_id={"subband": (s + d) % ns}, device_id_type=MESH)

    @pl.when(z > 0)
    def _():
        pl.semaphore_signal(barrier, inc=1, device_id={"facet": z - 1}, device_id_type=MESH)

    @pl.when(z < nf - 1)
    def _():
        pl.semaphore_signal(barrier, inc=1, device_id={"facet": z + 1}, device_id_type=MESH)

    has_left = jnp.where(z > 0, 1, 0)
    has_right = jnp.where(z < nf - 1, 1, 0)
    pl.semaphore_wait(barrier, ns - 1 + has_left + has_right)

    first.wait()
    cross = []
    for d in range(1, nx):
        c = remote(kernel, kern.at[s], ks.at[d], kr.at[d], "subband", (s + 2 * d) % ns)
        c.start()
        cross.append(c)
    near = remote(kernel, kern.at[s], ks.at[0], kr.at[0], "subband", mate)
    near.start()
    kern[s] = kernel[...]

    def add(n, k):
        loads[n].wait()
        part = jnp.dot(model_v[n], kern[k], preferred_element_type=F32)
        acc[...] = part if n == 0 else acc[...] + part

    for c in others + [seen_load]:
        c.wait()
    spec = spec_v[...]
    for c in range(chunks):
        ids_v[c] = ids[c // per:c // per + 1, c % per * CHUNK:(c % per + 1) * CHUNK]
    offset = z * subs
    grid[...] = jnp.zeros_like(grid)

    passed = []
    stores = []

    def predict_own():
        add(0, s)
        near.wait_recv()
        add(1, mate)
        for d in range(1, nx):
            src = (s + ns - 2 * d) % ns
            cross[d - 1].wait_recv()
            c = remote(kern.at[src], kern.at[src], ks.at[nx + d - 1], kr.at[nx + d - 1], "subband", mate)
            c.start()
            passed.append(c)
            add(2 * d, src)

    def predict():
        for d in range(1, nx):
            passed[d - 1].wait_recv()
            add(2 * d + 1, (mate + ns - 2 * d) % ns)
        pred[...] = acc[...].astype(BF16)
        stores.append(pltpu.make_async_copy(kern, kern_h, dsem.at[0]))
        stores[0].start()

    def right(i):
        return remote(r_out.at[i], r_in.at[i], rs.at[i], rr.at[i], "facet", z + 1)

    def left(i):
        return remote(l_out.at[i], l_in.at[i], ls.at[i], lr.at[i], "facet", z - 1)

    def out(m, c):
        at = pl.multiple_of(c * CHUNK, CHUNK)
        return pltpu.make_async_copy(done.at[m], residual.at[0, pl.ds(at, CHUNK)], osem.at[c])

    def swap(d, k):
        return remote(done.at[early + k], px.at[s * picks + k], ps.at[d - 1, k], pr.at[d - 1, k],
                      "subband", (s + d) % ns)

    def seen(c):
        mine = jnp.where(owners[c // per] == z, 1.0, 0.0).astype(F32)
        at = pl.multiple_of((c % per) * CHUNK, CHUNK)
        return obs_v[c // per, pl.ds(at, CHUNK), :].astype(F32) * mine

    def picked(c):
        column = jnp.broadcast_to(ids_v[c] - offset, (128, CHUNK)).T
        lanes = lax.broadcasted_iota(jnp.int32, (CHUNK, 128), 1)
        pick = jnp.concatenate(
            [(column == lanes + 128 * j).astype(F32).astype(BF16) for j in range(subs // 128)], axis=1
        )
        return jnp.dot(pick, pred[...], preferred_element_type=F32)

    def step(t, _, first):
        def now(m):
            if first:
                return jnp.logical_and(m >= 0, m < early)
            return jnp.logical_and(m < messages, m >= jnp.where(t >= early + EXTRA, 0, early))

        if first:
            @pl.when(t < early)
            def _():
                vals[t] = seen(t)
        else:
            @pl.when(t < early + picks)
            def _():
                vals[t] = picked(s * picks + t - early)

            @pl.when(jnp.logical_and(t >= early + picks, t < messages))
            def _():
                vals[t] = seen(t - picks) - picked(t - picks) * spec

        i = t - LAG * z
        @pl.when(now(i))
        def _():
            @pl.when(z == 0)
            def _():
                r_out[i] = vals[i].astype(BF16)

            @pl.when(z > 0)
            def _():
                right(i).wait_recv()
                r_out[i] = (vals[i] + r_in[i].astype(F32)).astype(BF16)

            @pl.when(z < nf - 1)
            def _():
                right(i).start()

        j = t - LAG * (nf - 1 - z)
        @pl.when(now(j))
        def _():
            @pl.when(z == nf - 1)
            def _():
                l_out[j] = vals[j].astype(BF16)

            @pl.when(z < nf - 1)
            def _():
                left(j).wait_recv()
                l_out[j] = (vals[j] + l_in[j].astype(F32)).astype(BF16)

            @pl.when(z > 0)
            def _():
                left(j).start()

        e = t - LAG * jnp.maximum(z, nf - 1 - z)
        @pl.when(now(e))
        def _():
            @pl.when(z == 0)
            def _():
                done[e] = l_out[e]

            @pl.when(z == nf - 1)
            def _():
                done[e] = r_out[e]

            @pl.when(jnp.logical_and(z > 0, z < nf - 1))
            def _():
                done[e] = (vals[e] + (r_in[e].astype(F32) + l_in[e].astype(F32))).astype(BF16)

        if not first:
            @pl.when(jnp.logical_and(e >= early, e < early + picks))
            def _():
                px[s * picks + e - early] = done[e]
                for d in range(1, ns):
                    swap(d, e - early).start()

            @pl.when(jnp.logical_and(e >= early + picks, e < messages))
            def _():
                out(e, e - picks).start()
                place = (lax.broadcasted_iota(jnp.int32, (subs, CHUNK), 0) == ids_v[e - picks] - offset)
                grid[...] += jnp.dot(place.astype(F32).astype(BF16), done[e], preferred_element_type=F32)

        return 0

    lax.fori_loop(0, early, functools.partial(step, first=True), 0)
    predict_own()
    lax.fori_loop(early, early + EXTRA, functools.partial(step, first=True), 0)
    predict()
    lax.fori_loop(early, messages + LAG * (nf - 1), functools.partial(step, first=False), 0)

    for d in range(1, ns):
        for k in range(picks):
            swap(d, k).wait_recv()
    for c in range(0, early, GROUP):
        for n in range(c, c + GROUP):
            done[n] = (done[n].astype(F32) - px[n].astype(F32) * spec).astype(BF16)
            out(n, n).start()
        row = jnp.concatenate([ids_v[n] for n in range(c, c + GROUP)], axis=1) - offset
        place = lax.broadcasted_iota(jnp.int32, (subs, GROUP * CHUNK), 0) == row
        rows = jnp.concatenate([done[n] for n in range(c, c + GROUP)], axis=0)
        grid[...] += jnp.dot(place.astype(F32).astype(BF16), rows, preferred_element_type=F32)

    share = subs // ns
    wsend[...] = (grid[...] * spec).astype(BF16)
    parts = []
    for d in range(1, ns):
        to = (s + d) % ns
        at = pl.multiple_of(to * share, share)
        c = remote(wsend.at[pl.ds(at, share)], wrecv.at[d - 1], ws.at[d - 1], wr.at[d - 1], "subband", to)
        c.start()
        parts.append(c)
    total = wsend[pl.ds(pl.multiple_of(s * share, share), share), :].astype(F32)
    for d in range(1, ns):
        parts[d - 1].wait_recv()
        total = total + wrecv[d - 1].astype(F32)
    total_v[...] = total
    stores.append(pltpu.make_async_copy(total_v, total_h, dsem.at[1]))
    stores[1].start()

    for c in [near] + cross + passed + parts:
        c.wait_send()

    def drain(i, _):
        @pl.when(z < nf - 1)
        def _():
            right(i).wait_send()

        @pl.when(z > 0)
        def _():
            left(i).wait_send()

        return 0

    lax.fori_loop(0, messages, drain, 0)
    for d in range(1, ns):
        for k in range(picks):
            swap(d, k).wait_send()
    for c in range(chunks):
        out(c if c < early else c + picks, c).wait()
    for c in stores:
        c.wait()


def finish(residual, total_h, kern_h, res_out, dirty, total_v, kern, dout, res_v, sem, ksem, dsem):
    ns, depth, _ = kern.shape
    loads = [pltpu.make_async_copy(kern_h.at[k], kern.at[k], ksem.at[k]) for k in range(ns)]
    first = pltpu.make_async_copy(total_h, total_v, sem.at[0])
    inward = pltpu.make_async_copy(residual, res_v, sem.at[1])
    outward = pltpu.make_async_copy(res_v, res_out, sem.at[2])
    first.start()
    for c in loads:
        c.start()
    inward.start()
    first.wait()
    total = total_v[...]
    inward.wait()
    outward.start()
    high = total.astype(BF16)
    low = (total - high.astype(F32)).astype(BF16)
    back = (((1,), (1,)), ((), ()))
    stores = []
    for k in range(ns):
        loads[k].wait()
        block = lax.dot_general(high, kern[k], back, preferred_element_type=F32)
        block += lax.dot_general(low, kern[k], back, preferred_element_type=F32)
        dout[k] = block.astype(BF16)
        c = pltpu.make_async_copy(dout.at[k], dirty.at[:, pl.ds(k * depth, depth)], dsem.at[k])
        c.start()
        stores.append(c)
    for c in stores:
        c.wait()
    outward.wait()


def local(nf, ns, model, kernel, spectrum, observed, subgrid_ids, owners):
    subs, pix = model.shape
    depth, width = kernel.shape
    spans, nblk = subgrid_ids.shape
    chunks = spans * nblk // CHUNK
    share = subs // ns
    dma = pltpu.SemaphoreType.DMA
    anywhere = pl.BlockSpec(memory_space=pl.ANY)
    early = chunks // 2
    picks = early // ns
    messages = chunks + picks
    flow = pltpu.VMEM((messages, CHUNK, width), BF16)
    residual, total, kern = pl.pallas_call(
        functools.partial(body, nf, ns),
        out_shape=(
            jax.ShapeDtypeStruct((1, spans * nblk, width), BF16),
            jax.ShapeDtypeStruct((share, width), F32),
            jax.ShapeDtypeStruct((ns, depth, width), BF16),
        ),
        in_specs=[anywhere] * 6,
        out_specs=(anywhere,) * 3,
        scratch_shapes=[
            pltpu.VMEM((depth, width), BF16),
            pltpu.VMEM((spans, nblk), jnp.int32),
            pltpu.SMEM(owners.shape, jnp.int32),
            pltpu.VMEM((1, width), F32),
            dma((4,)),
            pltpu.VMEM((ns, subs, depth), BF16),
            pltpu.VMEM((ns, depth, width), BF16),
            pltpu.VMEM((subs, width), F32),
            pltpu.VMEM((subs, width), BF16),
            pltpu.VMEM((messages, CHUNK, width), F32),
            flow, flow, flow, flow, flow,
            pltpu.VMEM((early, CHUNK, width), BF16),
            pltpu.VMEM((subs, width), F32),
            pltpu.VMEM((subs, width), BF16),
            pltpu.VMEM((ns - 1, share, width), BF16),
            pltpu.VMEM((share, width), F32),
            pltpu.VMEM((chunks, 1, CHUNK), jnp.int32),
            pltpu.VMEM(observed.shape[1:], BF16),
            dma,
            dma((ns,)),
            dma((ns,)), dma((ns,)),
            dma((messages,)), dma((messages,)), dma((messages,)), dma((messages,)),
            dma((ns - 1, picks)), dma((ns - 1, picks)),
            dma((ns - 1,)), dma((ns - 1,)),
            dma((chunks,)), dma((2,)),
        ],
        compiler_params=pltpu.CompilerParams(
            collective_id=0, has_side_effects=True, vmem_limit_bytes=60 * 1024 * 1024
        ),
        name="major_cycle",
    )(model, kernel, spectrum, observed, subgrid_ids, owners)
    return pl.pallas_call(
        finish,
        out_shape=(
            jax.ShapeDtypeStruct(residual.shape, BF16),
            jax.ShapeDtypeStruct((share, pix), BF16),
        ),
        in_specs=[anywhere] * 3,
        out_specs=(anywhere,) * 2,
        scratch_shapes=[
            pltpu.VMEM(total.shape, F32), pltpu.VMEM(kern.shape, BF16),
            pltpu.VMEM((ns, share, depth), BF16),
            pltpu.VMEM(residual.shape, BF16),
            dma((3,)), dma((ns,)), dma((ns,)),
        ],
        compiler_params=pltpu.CompilerParams(vmem_limit_bytes=60 * 1024 * 1024),
        name="back",
    )(residual, total, kern)


def solution(mesh):
    return jax.shard_map(
        functools.partial(local, mesh.shape["facet"], mesh.shape["subband"]),
        mesh=mesh,
        in_specs=(
            P(("groups", "facet"), None),
            P("subband", None),
            P(("groups", "subband"), None),
            P(("groups", "subband"), "facet", None, None),
            P("groups", None),
            P("groups"),
        ),
        out_specs=(P(("groups", "subband"), None, None), P(("groups", "facet", "subband"), None)),
        check_vma=False,
    )
```

```python
import functools

import jax
import jax.numpy as jnp
from jax import lax
from jax.experimental import pallas as pl
from jax.experimental.pallas import tpu as pltpu
from jax.sharding import PartitionSpec as P

MESH = pl.DeviceIdType.MESH
F32 = jnp.float32
BF16 = jnp.bfloat16
CHUNK = 128
GROUP = 4
LAG = 5
EXTRA = 5


def remote(src, dst, send, recv, axis, target):
    return pltpu.make_async_remote_copy(
        src_ref=src, dst_ref=dst, send_sem=send, recv_sem=recv,
        device_id={axis: target}, device_id_type=MESH,
    )


def body(nf, ns, model, kernel_h, spectrum, observed, ids_h, owners_h, residual, total_h, kern_h,
         kernel, ids, owners, spec_v, small,
         model_v, kern, acc, pred, vals, r_in, l_in, r_out, l_out, done, px, grid, wsend, wrecv, total_v,
         ids_v, obs_v, obsem, msem, ks, kr, rs, rr, ls, lr, ps, pr, ws, wr, osem, dsem):
    z = lax.axis_index("facet")
    s = lax.axis_index("subband")
    nx = ns // 2
    mate = s + 1 - 2 * (s % 2)
    subs, depth = model_v.shape[1], model_v.shape[2]
    spans, nblk = ids.shape
    per = nblk // CHUNK
    chunks = spans * per
    early = chunks // 2
    picks = early // ns
    messages = chunks + picks
    width = kernel.shape[1]

    first = pltpu.make_async_copy(kernel_h, kernel, small.at[0])
    first.start()
    others = [
        pltpu.make_async_copy(ids_h, ids, small.at[1]),
        pltpu.make_async_copy(owners_h, owners, small.at[2]),
        pltpu.make_async_copy(spectrum, spec_v, small.at[3]),
    ]
    for c in others:
        c.start()

    order = [s, mate]
    for d in range(1, nx):
        order += [(s + ns - 2 * d) % ns, (mate + ns - 2 * d) % ns]
    loads = []
    for n, k in enumerate(order):
        at = pl.multiple_of(k * depth, depth)
        loads.append(pltpu.make_async_copy(model.at[:, pl.ds(at, depth)], model_v.at[n], msem.at[n]))
        loads[-1].start()

    seen_load = pltpu.make_async_copy(observed.at[0], obs_v, obsem)
    seen_load.start()
    barrier = pltpu.get_barrier_semaphore()
    for d in range(1, ns):
        pl.semaphore_signal(barrier, inc=1, device_id={"subband": (s + d) % ns}, device_id_type=MESH)

    @pl.when(z > 0)
    def _():
        pl.semaphore_signal(barrier, inc=1, device_id={"facet": z - 1}, device_id_type=MESH)

    @pl.when(z < nf - 1)
    def _():
        pl.semaphore_signal(barrier, inc=1, device_id={"facet": z + 1}, device_id_type=MESH)

    has_left = jnp.where(z > 0, 1, 0)
    has_right = jnp.where(z < nf - 1, 1, 0)
    pl.semaphore_wait(barrier, ns - 1 + has_left + has_right)

    first.wait()
    half = depth // 2
    cross, direct = [], []
    for d in range(1, nx):
        c = remote(kernel.at[pl.ds(0, half)], kern.at[s, pl.ds(0, half)], ks.at[d], kr.at[d],
                   "subband", (s + 2 * d) % ns)
        c.start()
        cross.append(c)
    near = remote(kernel, kern.at[s], ks.at[0], kr.at[0], "subband", mate)
    near.start()
    for d in range(1, nx):
        for q, peer in enumerate((s, mate)):
            n = ns + 2 * (d - 1) + q
            c = remote(kernel.at[pl.ds(half, half)], kern.at[s, pl.ds(half, half)], ks.at[n], kr.at[n],
                       "subband", (peer + 2 * d) % ns)
            c.start()
            direct.append(c)
    kern[s] = kernel[...]

    def add(n, k):
        loads[n].wait()
        part = jnp.dot(model_v[n], kern[k], preferred_element_type=F32)
        acc[...] = part if n == 0 else acc[...] + part

    for c in others + [seen_load]:
        c.wait()
    spec = spec_v[...]
    for c in range(chunks):
        ids_v[c] = ids[c // per:c // per + 1, c % per * CHUNK:(c % per + 1) * CHUNK]
    offset = z * subs
    grid[...] = jnp.zeros_like(grid)

    passed = []
    stores = []

    def predict_own():
        add(0, s)
        near.wait_recv()
        add(1, mate)
        for d in range(1, nx):
            src = (s + ns - 2 * d) % ns
            cross[d - 1].wait_recv()
            c = remote(kern.at[src, pl.ds(0, half)], kern.at[src, pl.ds(0, half)], ks.at[nx + d - 1],
                       kr.at[nx + d - 1], "subband", mate)
            c.start()
            passed.append(c)

    def predict():
        for d in range(1, nx):
            direct[2 * d - 2].wait_recv()
            add(2 * d, (s + ns - 2 * d) % ns)
            passed[d - 1].wait_recv()
            direct[2 * d - 1].wait_recv()
            add(2 * d + 1, (mate + ns - 2 * d) % ns)
        pred[...] = acc[...].astype(BF16)
        stores.append(pltpu.make_async_copy(kern, kern_h, dsem.at[0]))
        stores[0].start()

    def right(i):
        return remote(r_out.at[i], r_in.at[i], rs.at[i], rr.at[i], "facet", z + 1)

    def left(i):
        return remote(l_out.at[i], l_in.at[i], ls.at[i], lr.at[i], "facet", z - 1)

    def out(m, c):
        at = pl.multiple_of(c * CHUNK, CHUNK)
        return pltpu.make_async_copy(done.at[m], residual.at[0, pl.ds(at, CHUNK)], osem.at[c])

    def swap(d, k):
        return remote(done.at[early + k], px.at[s * picks + k], ps.at[d - 1, k], pr.at[d - 1, k],
                      "subband", (s + d) % ns)

    def seen(c):
        mine = jnp.where(owners[c // per] == z, 1.0, 0.0).astype(F32)
        at = pl.multiple_of((c % per) * CHUNK, CHUNK)
        return obs_v[c // per, pl.ds(at, CHUNK), :].astype(F32) * mine

    def picked(c):
        column = jnp.broadcast_to(ids_v[c] - offset, (128, CHUNK)).T
        lanes = lax.broadcasted_iota(jnp.int32, (CHUNK, 128), 1)
        pick = jnp.concatenate(
            [(column == lanes + 128 * j).astype(F32).astype(BF16) for j in range(subs // 128)], axis=1
        )
        return jnp.dot(pick, pred[...], preferred_element_type=F32)

    def step(t, _, first):
        def now(m):
            if first:
                return jnp.logical_and(m >= 0, m < early)
            return jnp.logical_and(m < messages, m >= jnp.where(t >= early + EXTRA, 0, early))

        if first:
            @pl.when(t < early)
            def _():
                vals[t] = seen(t)
        else:
            @pl.when(t < early + picks)
            def _():
                vals[t] = picked(s * picks + t - early)

            @pl.when(jnp.logical_and(t >= early + picks, t < messages))
            def _():
                vals[t] = seen(t - picks) - picked(t - picks) * spec

        i = t - LAG * z
        @pl.when(now(i))
        def _():
            @pl.when(z == 0)
            def _():
                r_out[i] = vals[i].astype(BF16)

            @pl.when(z > 0)
            def _():
                right(i).wait_recv()
                r_out[i] = (vals[i] + r_in[i].astype(F32)).astype(BF16)

            @pl.when(z < nf - 1)
            def _():
                right(i).start()

        j = t - LAG * (nf - 1 - z)
        @pl.when(now(j))
        def _():
            @pl.when(z == nf - 1)
            def _():
                l_out[j] = vals[j].astype(BF16)

            @pl.when(z < nf - 1)
            def _():
                left(j).wait_recv()
                l_out[j] = (vals[j] + l_in[j].astype(F32)).astype(BF16)

            @pl.when(z > 0)
            def _():
                left(j).start()

        e = t - LAG * jnp.maximum(z, nf - 1 - z)
        @pl.when(now(e))
        def _():
            @pl.when(z == 0)
            def _():
                done[e] = l_out[e]

            @pl.when(z == nf - 1)
            def _():
                done[e] = r_out[e]

            @pl.when(jnp.logical_and(z > 0, z < nf - 1))
            def _():
                done[e] = (vals[e] + (r_in[e].astype(F32) + l_in[e].astype(F32))).astype(BF16)

        if not first:
            @pl.when(jnp.logical_and(e >= early, e < early + picks))
            def _():
                px[s * picks + e - early] = done[e]
                for d in range(1, ns):
                    swap(d, e - early).start()

            @pl.when(jnp.logical_and(e >= early + picks, e < messages))
            def _():
                out(e, e - picks).start()
                place = (lax.broadcasted_iota(jnp.int32, (subs, CHUNK), 0) == ids_v[e - picks] - offset)
                grid[...] += jnp.dot(place.astype(F32).astype(BF16), done[e], preferred_element_type=F32)

        return 0

    lax.fori_loop(0, early, functools.partial(step, first=True), 0)
    predict_own()
    lax.fori_loop(early, early + EXTRA, functools.partial(step, first=True), 0)
    predict()
    lax.fori_loop(early, messages + LAG * (nf - 1), functools.partial(step, first=False), 0)

    for d in range(1, ns):
        for k in range(picks):
            swap(d, k).wait_recv()
    for c in range(0, early, GROUP):
        for n in range(c, c + GROUP):
            done[n] = (done[n].astype(F32) - px[n].astype(F32) * spec).astype(BF16)
            out(n, n).start()
        row = jnp.concatenate([ids_v[n] for n in range(c, c + GROUP)], axis=1) - offset
        place = lax.broadcasted_iota(jnp.int32, (subs, GROUP * CHUNK), 0) == row
        rows = jnp.concatenate([done[n] for n in range(c, c + GROUP)], axis=0)
        grid[...] += jnp.dot(place.astype(F32).astype(BF16), rows, preferred_element_type=F32)

    share = subs // ns
    wsend[...] = (grid[...] * spec).astype(BF16)
    parts = []
    for d in range(1, ns):
        to = (s + d) % ns
        at = pl.multiple_of(to * share, share)
        c = remote(wsend.at[pl.ds(at, share)], wrecv.at[d - 1], ws.at[d - 1], wr.at[d - 1], "subband", to)
        c.start()
        parts.append(c)
    total = wsend[pl.ds(pl.multiple_of(s * share, share), share), :].astype(F32)
    for d in range(1, ns):
        parts[d - 1].wait_recv()
        total = total + wrecv[d - 1].astype(F32)
    total_v[...] = total
    stores.append(pltpu.make_async_copy(total_v, total_h, dsem.at[1]))
    stores[1].start()

    for c in [near] + cross + direct + passed + parts:
        c.wait_send()

    def drain(i, _):
        @pl.when(z < nf - 1)
        def _():
            right(i).wait_send()

        @pl.when(z > 0)
        def _():
            left(i).wait_send()

        return 0

    lax.fori_loop(0, messages, drain, 0)
    for d in range(1, ns):
        for k in range(picks):
            swap(d, k).wait_send()
    for c in range(chunks):
        out(c if c < early else c + picks, c).wait()
    for c in stores:
        c.wait()


def finish(residual, total_h, kern_h, res_out, dirty, total_v, kern, dout, res_v, sem, ksem, dsem):
    ns, depth, _ = kern.shape
    loads = [pltpu.make_async_copy(kern_h.at[k], kern.at[k], ksem.at[k]) for k in range(ns)]
    first = pltpu.make_async_copy(total_h, total_v, sem.at[0])
    inward = pltpu.make_async_copy(residual, res_v, sem.at[1])
    outward = pltpu.make_async_copy(res_v, res_out, sem.at[2])
    first.start()
    for c in loads:
        c.start()
    inward.start()
    first.wait()
    total = total_v[...]
    inward.wait()
    outward.start()
    high = total.astype(BF16)
    low = (total - high.astype(F32)).astype(BF16)
    back = (((1,), (1,)), ((), ()))
    stores = []
    for k in range(ns):
        loads[k].wait()
        block = lax.dot_general(high, kern[k], back, preferred_element_type=F32)
        block += lax.dot_general(low, kern[k], back, preferred_element_type=F32)
        dout[k] = block.astype(BF16)
        c = pltpu.make_async_copy(dout.at[k], dirty.at[:, pl.ds(k * depth, depth)], dsem.at[k])
        c.start()
        stores.append(c)
    for c in stores:
        c.wait()
    outward.wait()


def local(nf, ns, model, kernel, spectrum, observed, subgrid_ids, owners):
    subs, pix = model.shape
    depth, width = kernel.shape
    spans, nblk = subgrid_ids.shape
    chunks = spans * nblk // CHUNK
    share = subs // ns
    dma = pltpu.SemaphoreType.DMA
    anywhere = pl.BlockSpec(memory_space=pl.ANY)
    early = chunks // 2
    picks = early // ns
    messages = chunks + picks
    flow = pltpu.VMEM((messages, CHUNK, width), BF16)
    residual, total, kern = pl.pallas_call(
        functools.partial(body, nf, ns),
        out_shape=(
            jax.ShapeDtypeStruct((1, spans * nblk, width), BF16),
            jax.ShapeDtypeStruct((share, width), F32),
            jax.ShapeDtypeStruct((ns, depth, width), BF16),
        ),
        in_specs=[anywhere] * 6,
        out_specs=(anywhere,) * 3,
        scratch_shapes=[
            pltpu.VMEM((depth, width), BF16),
            pltpu.VMEM((spans, nblk), jnp.int32),
            pltpu.SMEM(owners.shape, jnp.int32),
            pltpu.VMEM((1, width), F32),
            dma((4,)),
            pltpu.VMEM((ns, subs, depth), BF16),
            pltpu.VMEM((ns, depth, width), BF16),
            pltpu.VMEM((subs, width), F32),
            pltpu.VMEM((subs, width), BF16),
            pltpu.VMEM((messages, CHUNK, width), F32),
            flow, flow, flow, flow, flow,
            pltpu.VMEM((early, CHUNK, width), BF16),
            pltpu.VMEM((subs, width), F32),
            pltpu.VMEM((subs, width), BF16),
            pltpu.VMEM((ns - 1, share, width), BF16),
            pltpu.VMEM((share, width), F32),
            pltpu.VMEM((chunks, 1, CHUNK), jnp.int32),
            pltpu.VMEM(observed.shape[1:], BF16),
            dma,
            dma((ns,)),
            dma((2 * ns,)), dma((2 * ns,)),
            dma((messages,)), dma((messages,)), dma((messages,)), dma((messages,)),
            dma((ns - 1, picks)), dma((ns - 1, picks)),
            dma((ns - 1,)), dma((ns - 1,)),
            dma((chunks,)), dma((2,)),
        ],
        compiler_params=pltpu.CompilerParams(
            collective_id=0, has_side_effects=True, vmem_limit_bytes=60 * 1024 * 1024
        ),
        name="major_cycle",
    )(model, kernel, spectrum, observed, subgrid_ids, owners)
    return pl.pallas_call(
        finish,
        out_shape=(
            jax.ShapeDtypeStruct(residual.shape, BF16),
            jax.ShapeDtypeStruct((share, pix), BF16),
        ),
        in_specs=[anywhere] * 3,
        out_specs=(anywhere,) * 2,
        scratch_shapes=[
            pltpu.VMEM(total.shape, F32), pltpu.VMEM(kern.shape, BF16),
            pltpu.VMEM((ns, share, depth), BF16),
            pltpu.VMEM(residual.shape, BF16),
            dma((3,)), dma((ns,)), dma((ns,)),
        ],
        compiler_params=pltpu.CompilerParams(vmem_limit_bytes=60 * 1024 * 1024),
        name="back",
    )(residual, total, kern)


def solution(mesh):
    return jax.shard_map(
        functools.partial(local, mesh.shape["facet"], mesh.shape["subband"]),
        mesh=mesh,
        in_specs=(
            P(("groups", "facet"), None),
            P("subband", None),
            P(("groups", "subband"), None),
            P(("groups", "subband"), "facet", None, None),
            P("groups", None),
            P("groups"),
        ),
        out_specs=(P(("groups", "subband"), None, None), P(("groups", "facet", "subband"), None)),
        check_vma=False,
    )
```

```python
import functools

import jax
import jax.numpy as jnp
from jax import lax
from jax.experimental import pallas as pl
from jax.experimental.pallas import tpu as pltpu
from jax.sharding import PartitionSpec as P

MESH = pl.DeviceIdType.MESH
F32 = jnp.float32
BF16 = jnp.bfloat16
CHUNK = 128
GROUP = 8
LAG = 5
EXTRA = 5


def remote(src, dst, send, recv, axis, target):
    return pltpu.make_async_remote_copy(
        src_ref=src, dst_ref=dst, send_sem=send, recv_sem=recv,
        device_id={axis: target}, device_id_type=MESH,
    )


def body(nf, ns, model, kernel_h, spectrum, observed, ids_h, owners_h, residual, total_h, kern_h,
         kernel, ids, owners, spec_v, small,
         model_v, kern, acc, pred, vals, r_in, l_in, r_out, l_out, done, px, grid, wsend, wrecv, total_v,
         ids_v, obs_v, obsem, msem, ks, kr, rs, rr, ls, lr, ps, pr, ws, wr, osem, dsem):
    z = lax.axis_index("facet")
    s = lax.axis_index("subband")
    nx = ns // 2
    mate = s + 1 - 2 * (s % 2)
    subs, depth = model_v.shape[1], model_v.shape[2]
    spans, nblk = ids.shape
    per = nblk // CHUNK
    chunks = spans * per
    early = chunks // 2
    picks = early // ns
    messages = chunks + picks
    width = kernel.shape[1]

    first = pltpu.make_async_copy(kernel_h, kernel, small.at[0])
    first.start()
    others = [
        pltpu.make_async_copy(ids_h, ids, small.at[1]),
        pltpu.make_async_copy(owners_h, owners, small.at[2]),
        pltpu.make_async_copy(spectrum, spec_v, small.at[3]),
    ]
    for c in others:
        c.start()

    order = [s, mate]
    for d in range(1, nx):
        order += [(s + ns - 2 * d) % ns, (mate + ns - 2 * d) % ns]
    loads = []
    for n, k in enumerate(order):
        at = pl.multiple_of(k * depth, depth)
        loads.append(pltpu.make_async_copy(model.at[:, pl.ds(at, depth)], model_v.at[n], msem.at[n]))
        loads[-1].start()

    seen_load = pltpu.make_async_copy(observed.at[0], obs_v, obsem)
    seen_load.start()
    barrier = pltpu.get_barrier_semaphore()
    for d in range(1, ns):
        pl.semaphore_signal(barrier, inc=1, device_id={"subband": (s + d) % ns}, device_id_type=MESH)

    @pl.when(z > 0)
    def _():
        pl.semaphore_signal(barrier, inc=1, device_id={"facet": z - 1}, device_id_type=MESH)

    @pl.when(z < nf - 1)
    def _():
        pl.semaphore_signal(barrier, inc=1, device_id={"facet": z + 1}, device_id_type=MESH)

    has_left = jnp.where(z > 0, 1, 0)
    has_right = jnp.where(z < nf - 1, 1, 0)
    pl.semaphore_wait(barrier, ns - 1 + has_left + has_right)

    first.wait()
    cross = []
    for d in range(1, nx):
        c = remote(kernel, kern.at[s], ks.at[d], kr.at[d], "subband", (s + 2 * d) % ns)
        c.start()
        cross.append(c)
    near = remote(kernel, kern.at[s], ks.at[0], kr.at[0], "subband", mate)
    near.start()
    kern[s] = kernel[...]

    def add(n, k):
        loads[n].wait()
        part = jnp.dot(model_v[n], kern[k], preferred_element_type=F32)
        acc[...] = part if n == 0 else acc[...] + part

    for c in others + [seen_load]:
        c.wait()
    spec = spec_v[...]
    for c in range(chunks):
        ids_v[c] = ids[c // per:c // per + 1, c % per * CHUNK:(c % per + 1) * CHUNK]
    offset = z * subs
    grid[...] = jnp.zeros_like(grid)

    passed = []
    stores = []

    def predict_own():
        add(0, s)
        near.wait_recv()
        add(1, mate)
        for d in range(1, nx):
            src = (s + ns - 2 * d) % ns
            cross[d - 1].wait_recv()
            c = remote(kern.at[src], kern.at[src], ks.at[nx + d - 1], kr.at[nx + d - 1], "subband", mate)
            c.start()
            passed.append(c)
            add(2 * d, src)

    def predict():
        for d in range(1, nx):
            passed[d - 1].wait_recv()
            add(2 * d + 1, (mate + ns - 2 * d) % ns)
        pred[...] = acc[...].astype(BF16)
        stores.append(pltpu.make_async_copy(kern, kern_h, dsem.at[0]))
        stores[0].start()

    def right(i):
        return remote(r_out.at[i], r_in.at[i], rs.at[i], rr.at[i], "facet", z + 1)

    def left(i):
        return remote(l_out.at[i], l_in.at[i], ls.at[i], lr.at[i], "facet", z - 1)

    def out(m, c):
        at = pl.multiple_of(c * CHUNK, CHUNK)
        return pltpu.make_async_copy(done.at[m], residual.at[0, pl.ds(at, CHUNK)], osem.at[c])

    def swap(d, k):
        return remote(done.at[early + k], px.at[s * picks + k], ps.at[d - 1, k], pr.at[d - 1, k],
                      "subband", (s + d) % ns)

    def seen(c):
        mine = jnp.where(owners[c // per] == z, 1.0, 0.0).astype(F32)
        at = pl.multiple_of((c % per) * CHUNK, CHUNK)
        return obs_v[c // per, pl.ds(at, CHUNK), :].astype(F32) * mine

    def picked(c):
        column = jnp.broadcast_to(ids_v[c] - offset, (128, CHUNK)).T
        lanes = lax.broadcasted_iota(jnp.int32, (CHUNK, 128), 1)
        pick = jnp.concatenate(
            [(column == lanes + 128 * j).astype(F32).astype(BF16) for j in range(subs // 128)], axis=1
        )
        return jnp.dot(pick, pred[...], preferred_element_type=F32)

    def step(t, _, first):
        def now(m):
            if first:
                return jnp.logical_and(m >= 0, m < early)
            return jnp.logical_and(m < messages, m >= jnp.where(t >= early + EXTRA, 0, early))

        if first:
            @pl.when(t < early)
            def _():
                vals[t] = seen(t)
        else:
            @pl.when(t < early + picks)
            def _():
                vals[t] = picked(s * picks + t - early)

            @pl.when(jnp.logical_and(t >= early + picks, t < messages))
            def _():
                vals[t] = seen(t - picks) - picked(t - picks) * spec

        i = t - LAG * z
        @pl.when(now(i))
        def _():
            @pl.when(z == 0)
            def _():
                r_out[i] = vals[i].astype(BF16)

            @pl.when(z > 0)
            def _():
                right(i).wait_recv()
                r_out[i] = (vals[i] + r_in[i].astype(F32)).astype(BF16)

            @pl.when(z < nf - 1)
            def _():
                right(i).start()

        j = t - LAG * (nf - 1 - z)
        @pl.when(now(j))
        def _():
            @pl.when(z == nf - 1)
            def _():
                l_out[j] = vals[j].astype(BF16)

            @pl.when(z < nf - 1)
            def _():
                left(j).wait_recv()
                l_out[j] = (vals[j] + l_in[j].astype(F32)).astype(BF16)

            @pl.when(z > 0)
            def _():
                left(j).start()

        e = t - LAG * jnp.maximum(z, nf - 1 - z)
        @pl.when(now(e))
        def _():
            @pl.when(z == 0)
            def _():
                done[e] = l_out[e]

            @pl.when(z == nf - 1)
            def _():
                done[e] = r_out[e]

            @pl.when(jnp.logical_and(z > 0, z < nf - 1))
            def _():
                done[e] = (vals[e] + (r_in[e].astype(F32) + l_in[e].astype(F32))).astype(BF16)

        if not first:
            @pl.when(jnp.logical_and(e >= early, e < early + picks))
            def _():
                px[s * picks + e - early] = done[e]
                for d in range(1, ns):
                    swap(d, e - early).start()

            @pl.when(jnp.logical_and(e >= early + picks, e < messages))
            def _():
                out(e, e - picks).start()
                place = (lax.broadcasted_iota(jnp.int32, (subs, CHUNK), 0) == ids_v[e - picks] - offset)
                grid[...] += jnp.dot(place.astype(F32).astype(BF16), done[e], preferred_element_type=F32)

        return 0

    lax.fori_loop(0, early, functools.partial(step, first=True), 0)
    predict_own()
    lax.fori_loop(early, early + EXTRA, functools.partial(step, first=True), 0)
    predict()
    lax.fori_loop(early, messages + LAG * (nf - 1), functools.partial(step, first=False), 0)

    for d in range(1, ns):
        for k in range(picks):
            swap(d, k).wait_recv()
    for c in range(0, early, GROUP):
        for n in range(c, c + GROUP):
            done[n] = (done[n].astype(F32) - px[n].astype(F32) * spec).astype(BF16)
            out(n, n).start()
        row = jnp.concatenate([ids_v[n] for n in range(c, c + GROUP)], axis=1) - offset
        place = lax.broadcasted_iota(jnp.int32, (subs, GROUP * CHUNK), 0) == row
        rows = jnp.concatenate([done[n] for n in range(c, c + GROUP)], axis=0)
        grid[...] += jnp.dot(place.astype(F32).astype(BF16), rows, preferred_element_type=F32)

    share = subs // ns
    wsend[...] = (grid[...] * spec).astype(BF16)
    parts = []
    for d in range(1, ns):
        to = (s + d) % ns
        at = pl.multiple_of(to * share, share)
        c = remote(wsend.at[pl.ds(at, share)], wrecv.at[d - 1], ws.at[d - 1], wr.at[d - 1], "subband", to)
        c.start()
        parts.append(c)
    for c in [near] + cross + passed:
        c.wait_send()

    def drain(i, _):
        @pl.when(z < nf - 1)
        def _():
            right(i).wait_send()

        @pl.when(z > 0)
        def _():
            left(i).wait_send()

        return 0

    lax.fori_loop(0, messages, drain, 0)
    for d in range(1, ns):
        for k in range(picks):
            swap(d, k).wait_send()
    for c in range(chunks):
        out(c if c < early else c + picks, c).wait()

    total = wsend[pl.ds(pl.multiple_of(s * share, share), share), :].astype(F32)
    for d in range(1, ns):
        parts[d - 1].wait_recv()
        total = total + wrecv[d - 1].astype(F32)
    total_v[...] = total
    stores.append(pltpu.make_async_copy(total_v, total_h, dsem.at[1]))
    stores[1].start()

    for c in parts:
        c.wait_send()
    for c in stores:
        c.wait()


def finish(residual, total_h, kern_h, res_out, dirty, total_v, kern, dout, res_v, sem, ksem, dsem):
    ns, depth, _ = kern.shape
    loads = [pltpu.make_async_copy(kern_h.at[k], kern.at[k], ksem.at[k]) for k in range(ns)]
    first = pltpu.make_async_copy(total_h, total_v, sem.at[0])
    inward = pltpu.make_async_copy(residual, res_v, sem.at[1])
    outward = pltpu.make_async_copy(res_v, res_out, sem.at[2])
    first.start()
    for c in loads:
        c.start()
    inward.start()
    first.wait()
    total = total_v[...]
    inward.wait()
    outward.start()
    high = total.astype(BF16)
    low = (total - high.astype(F32)).astype(BF16)
    back = (((1,), (1,)), ((), ()))
    stores = []
    for k in range(ns):
        loads[k].wait()
        block = lax.dot_general(high, kern[k], back, preferred_element_type=F32)
        block += lax.dot_general(low, kern[k], back, preferred_element_type=F32)
        dout[k] = block.astype(BF16)
        c = pltpu.make_async_copy(dout.at[k], dirty.at[:, pl.ds(k * depth, depth)], dsem.at[k])
        c.start()
        stores.append(c)
    for c in stores:
        c.wait()
    outward.wait()


def local(nf, ns, model, kernel, spectrum, observed, subgrid_ids, owners):
    subs, pix = model.shape
    depth, width = kernel.shape
    spans, nblk = subgrid_ids.shape
    chunks = spans * nblk // CHUNK
    share = subs // ns
    dma = pltpu.SemaphoreType.DMA
    anywhere = pl.BlockSpec(memory_space=pl.ANY)
    early = chunks // 2
    picks = early // ns
    messages = chunks + picks
    flow = pltpu.VMEM((messages, CHUNK, width), BF16)
    residual, total, kern = pl.pallas_call(
        functools.partial(body, nf, ns),
        out_shape=(
            jax.ShapeDtypeStruct((1, spans * nblk, width), BF16),
            jax.ShapeDtypeStruct((share, width), F32),
            jax.ShapeDtypeStruct((ns, depth, width), BF16),
        ),
        in_specs=[anywhere] * 6,
        out_specs=(anywhere,) * 3,
        scratch_shapes=[
            pltpu.VMEM((depth, width), BF16),
            pltpu.VMEM((spans, nblk), jnp.int32),
            pltpu.SMEM(owners.shape, jnp.int32),
            pltpu.VMEM((1, width), F32),
            dma((4,)),
            pltpu.VMEM((ns, subs, depth), BF16),
            pltpu.VMEM((ns, depth, width), BF16),
            pltpu.VMEM((subs, width), F32),
            pltpu.VMEM((subs, width), BF16),
            pltpu.VMEM((messages, CHUNK, width), F32),
            flow, flow, flow, flow, flow,
            pltpu.VMEM((early, CHUNK, width), BF16),
            pltpu.VMEM((subs, width), F32),
            pltpu.VMEM((subs, width), BF16),
            pltpu.VMEM((ns - 1, share, width), BF16),
            pltpu.VMEM((share, width), F32),
            pltpu.VMEM((chunks, 1, CHUNK), jnp.int32),
            pltpu.VMEM(observed.shape[1:], BF16),
            dma,
            dma((ns,)),
            dma((ns,)), dma((ns,)),
            dma((messages,)), dma((messages,)), dma((messages,)), dma((messages,)),
            dma((ns - 1, picks)), dma((ns - 1, picks)),
            dma((ns - 1,)), dma((ns - 1,)),
            dma((chunks,)), dma((2,)),
        ],
        compiler_params=pltpu.CompilerParams(
            collective_id=0, has_side_effects=True, vmem_limit_bytes=60 * 1024 * 1024
        ),
        name="major_cycle",
    )(model, kernel, spectrum, observed, subgrid_ids, owners)
    return pl.pallas_call(
        finish,
        out_shape=(
            jax.ShapeDtypeStruct(residual.shape, BF16),
            jax.ShapeDtypeStruct((share, pix), BF16),
        ),
        in_specs=[anywhere] * 3,
        out_specs=(anywhere,) * 2,
        scratch_shapes=[
            pltpu.VMEM(total.shape, F32), pltpu.VMEM(kern.shape, BF16),
            pltpu.VMEM((ns, share, depth), BF16),
            pltpu.VMEM(residual.shape, BF16),
            dma((3,)), dma((ns,)), dma((ns,)),
        ],
        compiler_params=pltpu.CompilerParams(vmem_limit_bytes=60 * 1024 * 1024),
        name="back",
    )(residual, total, kern)


def solution(mesh):
    return jax.shard_map(
        functools.partial(local, mesh.shape["facet"], mesh.shape["subband"]),
        mesh=mesh,
        in_specs=(
            P(("groups", "facet"), None),
            P("subband", None),
            P(("groups", "subband"), None),
            P(("groups", "subband"), "facet", None, None),
            P("groups", None),
            P("groups"),
        ),
        out_specs=(P(("groups", "subband"), None, None), P(("groups", "facet", "subband"), None)),
        check_vma=False,
    )
```
